32 devices in a mesh: section: 4 (over y, x), dp: 2 (over core), expert: 4 (over z).
Axes of the slice: x: 2, y: 2, z: 4, core: 2. Of those that a mesh axis runs over, the one named last changes fastest.
Arguments:
- stashed: bfloat16 [4, 1536, 2048], P('section', ('dp', 'expert')), may hold values from -6 to 6
- expert_ids: int32 [4, 1536, 8], P('section', ('dp', 'expert')), may hold values from 0 to 15, all different within a row; in each aligned block of 192 rows (0 to 191, 192 to 383, ..., all dimensions but the last counted through in order) at most 192 rows name the same one
- route_probs: float32 [4, 1536, 8], P('section', ('dp', 'expert')), may hold values from 0.02 to 1
- w_gate: bfloat16 [4, 16, 2048, 768], P('section', ('dp', 'expert')), may hold values from -0.125 to 0.125
- w_up: bfloat16 [4, 16, 2048, 768], P('section', ('dp', 'expert')), may hold values from -0.125 to 0.125
- w_down: bfloat16 [4, 16, 768, 2048], P('section', ('dp', 'expert')), may hold values from -0.21875 to 0.21875
Outputs:
- handed: bfloat16 [4, 1536, 2048], P('section', ('dp', 'expert'))
- balance: float32 [4], P('section')
The draws below stay inside these ranges and needn't reach their ends.
Inputs may be any that keep to these rules, and one draw needn't show every extreme that they name: `expert_ids`: each token names 8 different experts; among the tokens of one device (aligned blocks of 192 tokens) no expert is named more than 192 times, and in every draw some expert is named exactly 192 times in some block.
All inputs are finite; a program needn't handle non-finite values.
Results may differ from the reference program's by a relative error of at most 0.0032.
Values may be sent and summed in bfloat16 or wider, within the bound.
A program may use at most 128 MiB of HBM per device.

```python
import math
import jax
import jax.numpy as jnp
import numpy as np
from jax import lax

D = 2048
FF = 768
TOPK = 8
TOK_DEV = 192
SECTIONS = 4
TOKENS = 1536
EXPERTS = 16
CAP = 192


def block_scale(stream_key, dims, split, low, largest):
    def one(dim, parts):
        heights = jax.random.uniform(jax.random.fold_in(jax.random.fold_in(stream_key, 6), dim), (parts,), jnp.float32, low / len(split), largest / len(split))
        return jnp.repeat(jnp.exp(heights), dims[dim] // parts).reshape((-1,) + (1,) * (len(dims) - dim - 1))

    factor_of = one(*split[0])
    for cut in split[1:]:
        factor_of = factor_of * one(*cut)
    return factor_of


def assign_block(rng, own, number, rows, number_of, top, most, skew):
    ranking = jax.random.permutation(rng, number_of)
    heavy_load, ordinary = portions_of(number_of, rows * top, most, skew, True), portions_of(number_of, rows * top, most, skew, False)
    places = jnp.arange(number_of)

    def named(lengths, turn):
        used = int((lengths > 0).sum())
        fixed = max(1, used // 4)
        passed = fixed + (places - fixed + turn * (used - fixed)) % max(1, number_of - fixed)
        return jnp.zeros((number_of,), jnp.int32).at[ranking[jnp.where(places < fixed, places, passed)]].set(jnp.asarray(lengths, jnp.int32))

    lengths = jnp.where(number % 4 == 0, named(heavy_load, number // 4), named(ordinary, number - number // 4 - 1))
    mixed = jax.random.permutation(jax.random.fold_in(own, 3), number_of)
    donor, sink = mixed[0:number_of // 2 * 2:2], mixed[1:number_of // 2 * 2:2]
    slack = jnp.minimum(lengths[donor] - 1, most - lengths[sink]) // 2
    slack = jnp.where((donor == ranking[0]) | (sink == ranking[0]) | (lengths[sink] == 0), 0, jnp.maximum(slack, 0))
    passed = jax.random.randint(jax.random.fold_in(own, 4), (number_of // 2,), 0, 1 << 20) % (slack + 1)
    lengths = lengths.at[donor].add(-passed).at[sink].add(passed)
    members = jnp.searchsorted(jnp.cumsum(lengths), jnp.arange(rows * top), side="right").astype(jnp.int32)
    grid = members.reshape(top, rows).T
    grid = grid[jax.random.permutation(jax.random.fold_in(own, 1), rows)]
    turn = jax.random.randint(jax.random.fold_in(own, 2), (rows, 1), 0, top)
    return jnp.take_along_axis(grid, (jnp.arange(top)[None, :] + turn) % top, axis=1)


def portions_of(number_of, total, limit, skew, full):
    portions = [(1 << 20) // math.isqrt(standing ** skew) + 1 for standing in range(1, number_of + 1)]
    largest = limit if full else min(limit, max(-(-total // number_of), total * portions[0] // sum(portions)))
    least = 1 if total - largest >= number_of - 1 else 0
    given, spare = [largest] + [least] * (number_of - 1), total - largest - least * (number_of - 1)
    while spare > 0:
        candidates = [i for i in range(1, number_of) if given[i] < largest] or [i for i in range(1, number_of) if given[i] < limit]
        whole, budget = sum([portions[i] for i in candidates]), spare
        for i in candidates:
            more = min(limit - given[i], max(1, budget * portions[i] // whole), spare)
            given[i] = given[i] + more
            spare = spare - more
    return np.array(given)


def centred(stream_key, shape, spread, bound, split=(), kind=jnp.bfloat16):
    drawn = jax.random.normal(stream_key, shape, jnp.float32) * spread
    if len(split) > 0:
        drawn = block_scale(stream_key, shape, split, -0.22, 0.18) * drawn
    return jnp.clip(drawn, min=-bound, max=bound).astype(kind)


def setup_inputs(seed: int = 0) -> dict:
    streams_of = jax.random.split(jax.random.key(seed), 7)
    stashed = centred(streams_of[0], (SECTIONS, TOKENS, D), 1.0, 6.0, ((0, 4), (1, 8)))
    expert_ids_keys = jax.random.split(jax.random.fold_in(streams_of[1], 1), SECTIONS * TOKENS // TOK_DEV)
    expert_ids_turns = jax.random.permutation(jax.random.fold_in(streams_of[1], 3), SECTIONS * TOKENS // TOK_DEV)
    expert_ids = jax.vmap(lambda own, number: assign_block(jax.random.fold_in(streams_of[1], 2), own, number, TOK_DEV, EXPERTS, TOPK, CAP, 2))(expert_ids_keys, expert_ids_turns).reshape((SECTIONS, TOKENS, TOPK))
    route_probs = jnp.clip(jnp.exp(math.log(1.0) - 3.912023 * jax.random.uniform(streams_of[2], (SECTIONS, TOKENS, TOPK), jnp.float32) ** block_scale(streams_of[2], (SECTIONS, TOKENS, TOPK), ((0, 4), (1, 8)), -0.2, 0.2)), 0.02, 1.0)
    w_gate = centred(streams_of[3], (SECTIONS, EXPERTS, D, FF), D ** -0.5, 0.125, ((0, 4), (1, 8)))
    w_up = centred(streams_of[4], (SECTIONS, EXPERTS, D, FF), D ** -0.5, 0.125, ((0, 4), (1, 8)))
    w_down = centred(streams_of[5], (SECTIONS, EXPERTS, FF, D), FF ** -0.5, 0.21875, ((0, 4), (1, 8)))
    return {"stashed": stashed, "expert_ids": expert_ids, "route_probs": route_probs, "w_gate": w_gate, "w_up": w_up, "w_down": w_down}


def expert_ffn(rows, gate_w, up_w, down_w):
    gate_act = jnp.dot(rows, gate_w, preferred_element_type=jnp.float32)
    up_act = jnp.dot(rows, up_w, preferred_element_type=jnp.float32)
    hidden = (jax.nn.silu(gate_act) * up_act).astype(jnp.bfloat16)
    return jnp.dot(hidden, down_w, preferred_element_type=jnp.float32).astype(jnp.bfloat16)

def moe_layer(tokens_in, choice_ids, probs, gate_w, up_w, down_w):
    blocks = TOKENS // TOK_DEV
    inputs = tokens_in.astype(jnp.float32)
    normed = (inputs * lax.rsqrt(lax.optimization_barrier(jnp.mean(inputs * inputs, axis=-1, keepdims=True)) + 1e-06)).astype(jnp.bfloat16)
    normed_pad = jnp.concatenate([normed, jnp.zeros((1, D), jnp.bfloat16)], axis=0)
    grouped = choice_ids.reshape(blocks, TOK_DEV * TOPK)
    labels = jnp.arange(EXPERTS, dtype=jnp.int32)
    onehot = (grouped[:, :, None] == labels[None, None, :]).astype(jnp.int32)
    running = jnp.cumsum(onehot, axis=1).astype(jnp.int32)
    position = (lax.optimization_barrier(jnp.sum(running * onehot, axis=2)).astype(jnp.int32) - 1).reshape(TOKENS, TOPK)
    block_index = (jnp.arange(TOKENS, dtype=jnp.int32) // TOK_DEV)[:, None]
    slot_rows = (block_index * CAP + position).astype(jnp.int32)
    weights = probs / lax.optimization_barrier(jnp.sum(probs, axis=-1, keepdims=True))
    token_index = jnp.broadcast_to(jnp.arange(TOKENS, dtype=jnp.int32)[:, None], (TOKENS, TOPK)).astype(jnp.int32)
    slot_token = jnp.full((EXPERTS, blocks * CAP), TOKENS, jnp.int32).at[choice_ids, slot_rows].set(token_index)
    slot_weight = jnp.zeros((EXPERTS, blocks * CAP), weights.dtype).at[choice_ids, slot_rows].set(weights)

    def one_expert(mixture, packed):
        rows_idx, row_w, g_w, u_w, d_w = packed
        rows = normed_pad[rows_idx]
        out = expert_ffn(rows, g_w, u_w, d_w).astype(mixture.dtype)
        return (mixture.at[rows_idx].add(row_w[:, None].astype(mixture.dtype) * out), None)
    start = jnp.zeros((TOKENS + 1, D), inputs.dtype)
    mixture, unused = lax.scan(one_expert, start, (slot_token, slot_weight, gate_w, up_w, down_w))
    layer_out = (inputs + mixture[:TOKENS]).astype(jnp.bfloat16)
    counts = lax.optimization_barrier(jnp.sum(onehot, axis=(0, 1))).astype(weights.dtype)
    flat_hot = onehot.reshape(TOKENS * TOPK, EXPERTS).astype(weights.dtype)
    mass = jnp.dot(weights.reshape(-1), flat_hot, precision=lax.Precision.HIGHEST)
    loss = EXPERTS * jnp.sum(counts / (TOKENS * TOPK) * (mass / TOKENS))
    return (layer_out, loss)

def reference(stashed, expert_ids, route_probs, w_gate, w_up, w_down):
    layers = []
    losses = []
    for section_index in range(SECTIONS):
        layer_out, loss = moe_layer(stashed[section_index], expert_ids[section_index], route_probs[section_index], w_gate[section_index], w_up[section_index], w_down[section_index])
        layers.append(layer_out)
        losses.append(loss)
    stacked = jnp.stack(layers)
    handed = jnp.concatenate([stacked[-1:], stacked[:-1]], axis=0)
    return (handed, jnp.stack(losses).astype(jnp.float32))
```

```python
import functools

import jax
import jax.numpy as jnp
from jax import lax
from jax.experimental import pallas as pl
from jax.experimental.pallas import tpu as pltpu
from jax.sharding import PartitionSpec as P

MESH = pl.DeviceIdType.MESH
LANES = 128
SLOTS_MAX_BYTES = 48 << 20


def table_of(ids_t, probs_t, experts):
    weights = probs_t / jnp.sum(probs_t, axis=0, keepdims=True)
    labels = lax.broadcasted_iota(jnp.int32, (experts, ids_t.shape[1]), 0)
    table = jnp.zeros((experts, ids_t.shape[1]), jnp.float32)
    for k in range(ids_t.shape[0]):
        table = table + jnp.where(labels == ids_t[k : k + 1, :], weights[k : k + 1, :], 0.0)
    return table


def column_of(table, expert, rows):
    labels = lax.broadcasted_iota(jnp.int32, table.shape, 0)
    row = jnp.sum(jnp.where(labels == expert, table, 0.0), axis=0, keepdims=True)
    shape = (rows, table.shape[1])
    diagonal = lax.broadcasted_iota(jnp.int32, shape, 0) == lax.broadcasted_iota(jnp.int32, shape, 1)
    return jnp.sum(jnp.where(diagonal, row, 0.0), axis=1, keepdims=True)


def layer_kernel(
    n, sections, local, experts, tile,
    x_ref, ids_ref, probs_ref, wg_hbm, wu_hbm, wd_hbm,
    handed_ref, loss_ref,
    xg, cf, wg, wu, wd, hid, part, sib, red, got, out,
    w_sem, xs_sem, xr_sem, cs_sem, cr_sem, fs_sem, gs_sem,
    ps_sem, pr_sem, rs_sem, rr_sem, os_sem, or_sem,
):
    rows, width = x_ref.shape
    units = wg.shape[2]
    sec = lax.axis_index("section")
    c = lax.axis_index("dp")
    z = lax.axis_index("expert")
    other = 1 - c
    after = lax.rem(sec + 1, sections)
    before = lax.rem(sec + sections - 1, sections)
    me = c * n + z

    loads = []
    for number, (source, target) in enumerate(((wg_hbm, wg), (wu_hbm, wu), (wd_hbm, wd))):
        load = pltpu.make_async_copy(source, target, w_sem.at[number])
        load.start()
        loads.append(load)

    barrier = pltpu.get_barrier_semaphore()
    pl.semaphore_signal(barrier, inc=1, device_id=(sec, other, z), device_id_type=MESH)
    pl.semaphore_signal(barrier, inc=1, device_id=(after, c, z), device_id_type=MESH)
    pl.semaphore_signal(barrier, inc=1, device_id=(before, c, z), device_id_type=MESH)
    for step in range(1, n):
        pl.semaphore_signal(
            barrier, inc=1, device_id=(sec, c, lax.rem(z + step, n)), device_id_type=MESH
        )

    values = x_ref[...].astype(jnp.float32)
    scale = lax.rsqrt(jnp.mean(values * values, axis=-1, keepdims=True) + 1e-06)
    xg[z, c] = (values * scale).astype(jnp.bfloat16)
    cf[z, c] = table_of(ids_ref[...], probs_ref[...], experts)
    pl.semaphore_wait(barrier, n + 2)

    def pair(b, target, x_send, c_send):
        slot = (b, c)
        return (
            pltpu.make_async_remote_copy(
                src_ref=xg.at[slot], dst_ref=xg.at[slot],
                send_sem=x_send, recv_sem=xr_sem.at[slot],
                device_id=target, device_id_type=MESH,
            ),
            pltpu.make_async_remote_copy(
                src_ref=cf.at[slot], dst_ref=cf.at[slot],
                send_sem=c_send, recv_sem=cr_sem.at[slot],
                device_id=target, device_id_type=MESH,
            ),
        )

    def up(b):
        return pair(b, (sec, c, z + 1), xs_sem.at[b, 0], cs_sem.at[b, 0])

    def down(b):
        return pair(b, (sec, c, z - 1), xs_sem.at[b, 1], cs_sem.at[b, 1])

    def across(b):
        return pair(b, (sec, other, z), fs_sem.at[b], gs_sem.at[b])

    def goes_up(b):
        return (b <= z) & (z < n - 1)

    def goes_down(b):
        return (b >= z) & (z > 0)

    def start_all(copies):
        for copy in copies:
            copy.start()

    def arrived(b, side):
        slot = (b, side)
        pltpu.make_async_remote_copy(
            src_ref=xg.at[slot], dst_ref=xg.at[slot], send_sem=fs_sem.at[0],
            recv_sem=xr_sem.at[slot], device_id=(sec, other, z), device_id_type=MESH,
        ).wait_recv()
        pltpu.make_async_remote_copy(
            src_ref=cf.at[slot], dst_ref=cf.at[slot], send_sem=gs_sem.at[0],
            recv_sem=cr_sem.at[slot], device_id=(sec, other, z), device_id_type=MESH,
        ).wait_recv()

    def forward(b):
        @pl.when(goes_up(b))
        def _():
            start_all(up(b))

        @pl.when(goes_down(b))
        def _():
            start_all(down(b))

        start_all(across(b))

    mirrored = z // (n // 2)
    near = z + mirrored * (n - 1 - 2 * z)

    def block_at(i):
        if i == 0:
            place = near
        else:
            step = (i + 1) // 2
            early = near - step if i % 2 else near + step
            inside = (i <= 2 * near).astype(jnp.int32)
            place = inside * early + (1 - inside) * i
        return place + mirrored * (n - 1 - 2 * place)

    def to_sibling(b):
        return pltpu.make_async_remote_copy(
            src_ref=part.at[b, other], dst_ref=sib.at[b],
            send_sem=ps_sem.at[b], recv_sem=pr_sem.at[b],
            device_id=(sec, other, z), device_id_type=MESH,
        )

    def to_owner(b):
        return pltpu.make_async_remote_copy(
            src_ref=red.at[b], dst_ref=got.at[z],
            send_sem=rs_sem.at[b], recv_sem=rr_sem.at[z],
            device_id=(sec, c, b), device_id_type=MESH,
        )

    forward(z)
    for i in range(n):
        b = block_at(i)
        if i > 0:
            arrived(b, c)
            forward(b)
        arrived(b, other)
        if i == 0:
            loads[0].wait()
            loads[1].wait()
        tokens = xg[b].reshape(2 * rows, width)
        for e in range(local):
            expert = me * local + e
            weight = jnp.concatenate(
                [column_of(cf[b, side], expert, rows) for side in range(2)], axis=0
            )

            @pl.loop(0, units // tile)
            def _(j):
                columns = pl.ds(pl.multiple_of(j * tile, tile), tile)
                gate = jnp.dot(tokens, wg[e, :, columns], preferred_element_type=jnp.float32)
                lift = jnp.dot(tokens, wu[e, :, columns], preferred_element_type=jnp.float32)
                kept = pl.ds(pl.multiple_of(e * units + j * tile, tile), tile)
                hid[:, kept] = (jax.nn.silu(gate) * lift * weight).astype(jnp.bfloat16)

        if i == 0:
            loads[2].wait()
        hidden = hid[...]

        @pl.loop(0, width // tile)
        def _(j):
            columns = pl.ds(pl.multiple_of(j * tile, tile), tile)
            result = jnp.dot(hidden, wd[:, columns], preferred_element_type=jnp.float32)
            part[b, :, :, columns] = result.astype(jnp.bfloat16).reshape(2, rows, tile)

        copy = to_sibling(b)
        copy.start()
        copy.wait_recv()
        red[b] = (part[b, c].astype(jnp.float32) + sib[b].astype(jnp.float32)).astype(jnp.bfloat16)
        if i > 0:
            to_owner(b).start()

    total = jnp.zeros((experts, cf.shape[3]), jnp.float32)
    chosen = jnp.zeros((experts, cf.shape[3]), jnp.float32)
    for b in range(n):
        for side in range(2):
            total = total + cf[b, side]
            chosen = chosen + (cf[b, side] > 0.0).astype(jnp.float32)
    count = jnp.sum(chosen[:, :rows], axis=1, keepdims=True)
    mass = jnp.sum(total[:, :rows], axis=1, keepdims=True)
    tokens_all = 2 * n * rows
    picks = tokens_all * ids_ref.shape[0]
    loss = experts * jnp.sum(count / picks * (mass / tokens_all), axis=0, keepdims=True)
    loss_ref[...] = jnp.broadcast_to(loss, loss_ref.shape)

    for step in range(1, n):
        b = lax.rem(z + step, n)
        pltpu.make_async_remote_copy(
            src_ref=red.at[b], dst_ref=got.at[b], send_sem=rs_sem.at[b], recv_sem=rr_sem.at[b],
            device_id=(sec, c, b), device_id_type=MESH,
        ).wait_recv()
    finals = []
    chunks = os_sem.shape[0]
    height = rows // chunks
    for k in range(chunks):
        span = pl.ds(k * height, height)
        row = x_ref[span, :].astype(jnp.float32) + red[z, span, :].astype(jnp.float32)
        for step in range(1, n):
            row = row + got[lax.rem(z + step, n), span, :].astype(jnp.float32)
        out[span, :] = row.astype(jnp.bfloat16)
        copy = pltpu.make_async_remote_copy(
            src_ref=out.at[span, :], dst_ref=handed_ref.at[span, :],
            send_sem=os_sem.at[k], recv_sem=or_sem.at[k],
            device_id=(after, c, z), device_id_type=MESH,
        )
        copy.start()
        finals.append(copy)

    for b in range(n):
        @pl.when(goes_up(b))
        def _():
            for copy in up(b):
                copy.wait_send()

        @pl.when(goes_down(b))
        def _():
            for copy in down(b):
                copy.wait_send()

        for copy in across(b):
            copy.wait_send()
        to_sibling(b).wait_send()
    for step in range(1, n):
        to_owner(lax.rem(z + step, n)).wait_send()
    for copy in finals:
        copy.wait()


def by_kernel(tokens_in, ids, probs, gate_w, up_w, down_w):
    n = lax.axis_size("expert")
    sections = lax.axis_size("section")
    local, width, units = gate_w.shape
    rows, top = ids.shape
    experts = 2 * n * local
    lanes = -(-rows // LANES) * LANES
    ids_t = jnp.pad(ids.T, ((0, 0), (0, lanes - rows)), constant_values=-1)
    probs_t = jnp.pad(probs.T, ((0, 0), (0, lanes - rows)), constant_values=1.0)
    tile = 256 if units % 256 == 0 and width % 256 == 0 else 128
    chunks = 4 if rows % 64 == 0 else 1
    dma = pltpu.SemaphoreType.DMA
    block = pltpu.VMEM((n, rows, width), jnp.bfloat16)
    handed, loss = pl.pallas_call(
        functools.partial(layer_kernel, n, sections, local, experts, tile),
        out_shape=(
            jax.ShapeDtypeStruct((rows, width), jnp.bfloat16),
            jax.ShapeDtypeStruct((8, LANES), jnp.float32),
        ),
        in_specs=[pl.BlockSpec(memory_space=pltpu.VMEM)] * 3 + [pl.BlockSpec(memory_space=pl.ANY)] * 3,
        out_specs=(pl.BlockSpec(memory_space=pl.ANY), pl.BlockSpec(memory_space=pltpu.VMEM)),
        scratch_shapes=[
            pltpu.VMEM((n, 2, rows, width), jnp.bfloat16),
            pltpu.VMEM((n, 2, experts, lanes), jnp.float32),
            pltpu.VMEM((local, width, units), jnp.bfloat16),
            pltpu.VMEM((local, width, units), jnp.bfloat16),
            pltpu.VMEM((local * units, width), jnp.bfloat16),
            pltpu.VMEM((2 * rows, local * units), jnp.bfloat16),
            pltpu.VMEM((n, 2, rows, width), jnp.bfloat16),
            block, block, block,
            pltpu.VMEM((rows, width), jnp.bfloat16),
            dma((3,)),
            dma((n, 2)), dma((n, 2)), dma((n, 2)), dma((n, 2)), dma((n,)), dma((n,)),
            dma((n,)), dma((n,)), dma((n,)), dma((n,)), dma((chunks,)), dma((chunks,)),
        ],
        compiler_params=pltpu.CompilerParams(
            collective_id=0, has_side_effects=True, vmem_limit_bytes=58 << 20
        ),
    )(tokens_in, ids_t, probs_t, gate_w, up_w, down_w.reshape(local * units, width))
    return handed, loss[0, :1]


def by_collectives(tokens_in, ids, probs, gate_w, up_w, down_w):
    axes = ("dp", "expert")
    local = gate_w.shape[0]
    groups = lax.axis_size("dp") * lax.axis_size("expert")
    rows, top = ids.shape
    experts = groups * local
    inputs = tokens_in.astype(jnp.float32)
    normed = (inputs * lax.rsqrt(jnp.mean(inputs * inputs, axis=-1, keepdims=True) + 1e-06)).astype(
        jnp.bfloat16
    )
    table = table_of(ids.T, probs.T, experts)
    tables = lax.all_gather(table, axes)
    gathered = lax.all_gather(normed, axes, tiled=True)
    first = lax.axis_index(axes) * local
    mine = lax.dynamic_slice_in_dim(tables, first, local, axis=1)

    def one_block(packed):
        tokens, weight = packed
        mixed = jnp.zeros(tokens.shape, jnp.float32)
        for e in range(local):
            gate = jnp.dot(tokens, gate_w[e], preferred_element_type=jnp.float32)
            lift = jnp.dot(tokens, up_w[e], preferred_element_type=jnp.float32)
            hidden = (jax.nn.silu(gate) * lift).astype(jnp.bfloat16)
            result = jnp.dot(hidden, down_w[e], preferred_element_type=jnp.float32)
            mixed = mixed + weight[e][:, None] * result
        return mixed.astype(jnp.bfloat16)

    partial = lax.map(one_block, (gathered.reshape(groups, rows, -1), mine))
    spread = lax.all_to_all(partial, axes, split_axis=0, concat_axis=0, tiled=True)
    mixture = jnp.sum(spread.astype(jnp.float32), axis=0)
    layer_out = (inputs + mixture).astype(jnp.bfloat16)
    counts = jnp.sum((tables > 0.0).astype(jnp.float32), axis=(0, 2))
    mass = jnp.sum(tables, axis=(0, 2))
    tokens_all = groups * rows
    loss = experts * jnp.sum(counts / (tokens_all * top) * (mass / tokens_all))
    sections = lax.axis_size("section")
    handed = lax.ppermute(layer_out, "section", [(s, (s + 1) % sections) for s in range(sections)])
    return handed, loss.reshape(1)


def per_device(stashed, expert_ids, route_probs, w_gate, w_up, w_down):
    n = lax.axis_size("expert")
    slots = 8 * n * stashed.shape[1] * stashed.shape[2] * stashed.dtype.itemsize
    weights = 3 * w_gate.size * w_gate.dtype.itemsize
    fits = slots + weights <= SLOTS_MAX_BYTES
    even = lax.axis_size("dp") == 2 and n % 2 == 0 and lax.axis_size("section") > 2
    layer = by_kernel if fits and even else by_collectives
    handed, loss = layer(stashed[0], expert_ids[0], route_probs[0], w_gate[0], w_up[0], w_down[0])
    return handed[None], loss


def solution(mesh):
    placed = P("section", ("dp", "expert"), None)
    weights = P("section", ("dp", "expert"), None, None)
    return jax.shard_map(
        per_device,
        mesh=mesh,
        in_specs=(placed, placed, placed, weights, weights, weights),
        out_specs=(placed, P("section")),
        check_vma=False,
    )
```

```python
import functools

import jax
import jax.numpy as jnp
from jax import lax
from jax.experimental import pallas as pl
from jax.experimental.pallas import tpu as pltpu
from jax.sharding import PartitionSpec as P

MESH = pl.DeviceIdType.MESH
SLOTS_MAX_BYTES = 48 << 20


def table_of(ids_t, probs_t, experts):
    weights = probs_t / jnp.sum(probs_t, axis=0, keepdims=True)
    labels = lax.broadcasted_iota(jnp.int32, (experts, ids_t.shape[1]), 0)
    table = jnp.zeros((experts, ids_t.shape[1]), jnp.float32)
    for k in range(ids_t.shape[0]):
        table = table + jnp.where(labels == ids_t[k : k + 1, :], weights[k : k + 1, :], 0.0)
    return table


def column_of(table, expert, rows):
    labels = lax.broadcasted_iota(jnp.int32, table.shape, 0)
    row = jnp.sum(jnp.where(labels == expert, table, 0.0), axis=0, keepdims=True)
    shape = (rows, table.shape[1])
    diagonal = lax.broadcasted_iota(jnp.int32, shape, 0) == lax.broadcasted_iota(jnp.int32, shape, 1)
    return jnp.sum(jnp.where(diagonal, row, 0.0), axis=1, keepdims=True)


def layer_kernel(
    n, sections, local, experts, tile,
    x_ref, ids_ref, probs_ref, wg_hbm, wu_hbm, wd_hbm,
    handed_ref, loss_ref,
    xg, cf, wg, wu, wd, hid, part, sib, red, got, xprev,
    w_sem, xs_sem, xr_sem, cs_sem, cr_sem, fs_sem, gs_sem,
    ps_sem, pr_sem, rs_sem, rr_sem, os_sem, or_sem,
):
    rows, width = x_ref.shape
    units = wg.shape[2]
    chunks, span = part.shape[1], part.shape[4]
    sec = lax.axis_index("section")
    c = lax.axis_index("dp")
    z = lax.axis_index("expert")
    other = 1 - c
    after = lax.rem(sec + 1, sections)
    before = lax.rem(sec + sections - 1, sections)
    me = c * n + z

    loads = []
    for number, (source, target) in enumerate(((wg_hbm, wg), (wu_hbm, wu), (wd_hbm, wd))):
        load = pltpu.make_async_copy(source, target, w_sem.at[number])
        load.start()
        loads.append(load)

    barrier = pltpu.get_barrier_semaphore()
    pl.semaphore_signal(barrier, inc=1, device_id=(sec, other, z), device_id_type=MESH)
    for b in range(n):
        pl.semaphore_signal(barrier, inc=1, device_id=(before, c, b), device_id_type=MESH)
    for step in range(1, n):
        pl.semaphore_signal(
            barrier, inc=1, device_id=(sec, c, lax.rem(z + step, n)), device_id_type=MESH
        )

    values = x_ref[...].astype(jnp.float32)
    scale = lax.rsqrt(jnp.mean(values * values, axis=-1, keepdims=True) + 1e-06)
    xg[z, c] = (values * scale).astype(jnp.bfloat16)
    cf[z, c] = table_of(ids_ref[...], probs_ref[...], experts)
    pl.semaphore_wait(barrier, 2 * n)

    def pair(b, target, x_send, c_send):
        slot = (b, c)
        return (
            pltpu.make_async_remote_copy(
                src_ref=xg.at[slot], dst_ref=xg.at[slot],
                send_sem=x_send, recv_sem=xr_sem.at[slot],
                device_id=target, device_id_type=MESH,
            ),
            pltpu.make_async_remote_copy(
                src_ref=cf.at[slot], dst_ref=cf.at[slot],
                send_sem=c_send, recv_sem=cr_sem.at[slot],
                device_id=target, device_id_type=MESH,
            ),
        )

    def up(b):
        return pair(b, (sec, c, z + 1), xs_sem.at[b, 0], cs_sem.at[b, 0])

    def down(b):
        return pair(b, (sec, c, z - 1), xs_sem.at[b, 1], cs_sem.at[b, 1])

    def across(b):
        return pair(b, (sec, other, z), fs_sem.at[b], gs_sem.at[b])

    def goes_up(b):
        return (b <= z) & (z < n - 1)

    def goes_down(b):
        return (b >= z) & (z > 0)

    def start_all(copies):
        for copy in copies:
            copy.start()

    def arrived(b, side):
        slot = (b, side)
        pltpu.make_async_remote_copy(
            src_ref=xg.at[slot], dst_ref=xg.at[slot], send_sem=fs_sem.at[0],
            recv_sem=xr_sem.at[slot], device_id=(sec, other, z), device_id_type=MESH,
        ).wait_recv()
        pltpu.make_async_remote_copy(
            src_ref=cf.at[slot], dst_ref=cf.at[slot], send_sem=gs_sem.at[0],
            recv_sem=cr_sem.at[slot], device_id=(sec, other, z), device_id_type=MESH,
        ).wait_recv()

    def forward(b):
        @pl.when(goes_up(b))
        def _():
            start_all(up(b))

        @pl.when(goes_down(b))
        def _():
            start_all(down(b))

        start_all(across(b))

    mirrored = z // (n // 2)
    near = z + mirrored * (n - 1 - 2 * z)

    def block_at(i):
        if i == 0:
            place = near
        else:
            step = (i + 1) // 2
            early = near - step if i % 2 else near + step
            inside = (i <= 2 * near).astype(jnp.int32)
            place = inside * early + (1 - inside) * i
        return place + mirrored * (n - 1 - 2 * place)

    def to_sibling(b, q):
        return pltpu.make_async_remote_copy(
            src_ref=part.at[b, q, other], dst_ref=sib.at[b, q],
            send_sem=ps_sem.at[b, q], recv_sem=pr_sem.at[b, q],
            device_id=(sec, other, z), device_id_type=MESH,
        )

    def to_next(b, q):
        return pltpu.make_async_remote_copy(
            src_ref=red.at[b, q], dst_ref=got.at[z, q],
            send_sem=rs_sem.at[b, q], recv_sem=rr_sem.at[z, q],
            device_id=(after, c, b), device_id_type=MESH,
        )

    def finish(b, q):
        to_sibling(b, q).wait_recv()
        red[b, q] = (part[b, q, c].astype(jnp.float32) + sib[b, q].astype(jnp.float32)).astype(
            jnp.bfloat16
        )
        to_next(b, q).start()

    residual = pltpu.make_async_remote_copy(
        src_ref=x_ref, dst_ref=xprev, send_sem=os_sem, recv_sem=or_sem,
        device_id=(after, c, z), device_id_type=MESH,
    )
    pending = None
    forward(z)
    residual.start()
    for i in range(n):
        b = block_at(i)
        if i > 0:
            arrived(b, c)
            forward(b)
        arrived(b, other)
        if i == 0:
            loads[0].wait()
            loads[1].wait()
        tokens = xg[b].reshape(2 * rows, width)
        for e in range(local):
            expert = me * local + e
            weight = jnp.concatenate(
                [column_of(cf[b, side], expert, rows) for side in range(2)], axis=0
            )

            @pl.loop(0, units // tile)
            def _(j):
                columns = pl.ds(pl.multiple_of(j * tile, tile), tile)
                gate = jnp.dot(tokens, wg[e, :, columns], preferred_element_type=jnp.float32)
                lift = jnp.dot(tokens, wu[e, :, columns], preferred_element_type=jnp.float32)
                kept = pl.ds(pl.multiple_of(e * units + j * tile, tile), tile)
                hid[:, kept] = (jax.nn.silu(gate) * lift * weight).astype(jnp.bfloat16)

            if pending is not None:
                finish(*pending)
                pending = None

        if i == 0:
            loads[2].wait()
        hidden = hid[...]

        for q in range(chunks):

            @pl.loop(0, span // tile)
            def _(j):
                source = pl.ds(pl.multiple_of(q * span + j * tile, tile), tile)
                columns = pl.ds(pl.multiple_of(j * tile, tile), tile)
                result = jnp.dot(hidden, wd[:, source], preferred_element_type=jnp.float32)
                part[b, q, :, :, columns] = result.astype(jnp.bfloat16).reshape(2, rows, tile)

            to_sibling(b, q).start()
            if pending is not None:
                finish(*pending)
            pending = (b, q)

    finish(*pending)

    total = jnp.zeros((experts, cf.shape[3]), jnp.float32)
    chosen = jnp.zeros((experts, cf.shape[3]), jnp.float32)
    for b in range(n):
        for side in range(2):
            total = total + cf[b, side]
            chosen = chosen + (cf[b, side] > 0.0).astype(jnp.float32)
    count = jnp.sum(chosen, axis=1, keepdims=True)
    mass = jnp.sum(total, axis=1, keepdims=True)
    tokens_all = 2 * n * rows
    picks = tokens_all * ids_ref.shape[0]
    loss_ref[0] = experts * jnp.sum(count / picks * (mass / tokens_all))

    residual.wait_recv()
    for q in range(chunks):
        columns = pl.ds(q * span, span)
        row = xprev[:, columns].astype(jnp.float32)
        for b in range(n):
            pltpu.make_async_remote_copy(
                src_ref=red.at[b, q], dst_ref=got.at[b, q],
                send_sem=rs_sem.at[b, q], recv_sem=rr_sem.at[b, q],
                device_id=(after, c, b), device_id_type=MESH,
            ).wait_recv()
            row = row + got[b, q].astype(jnp.float32)
        handed_ref[:, columns] = row.astype(jnp.bfloat16)

    residual.wait_send()
    for b in range(n):
        @pl.when(goes_up(b))
        def _():
            for copy in up(b):
                copy.wait_send()

        @pl.when(goes_down(b))
        def _():
            for copy in down(b):
                copy.wait_send()

        for copy in across(b):
            copy.wait_send()
        for q in range(chunks):
            to_sibling(b, q).wait_send()
            to_next(b, q).wait_send()


def by_kernel(tokens_in, ids, probs, gate_w, up_w, down_w):
    n = lax.axis_size("expert")
    sections = lax.axis_size("section")
    local, width, units = gate_w.shape
    rows, top = ids.shape
    experts = 2 * n * local
    tile = 256 if units % 256 == 0 and width % 256 == 0 else 128
    chunks = 4 if width % (4 * tile) == 0 else 1
    span = width // chunks
    dma = pltpu.SemaphoreType.DMA
    block = pltpu.VMEM((n, chunks, rows, span), jnp.bfloat16)
    handed, loss = pl.pallas_call(
        functools.partial(layer_kernel, n, sections, local, experts, tile),
        out_shape=(
            jax.ShapeDtypeStruct((rows, width), jnp.bfloat16),
            jax.ShapeDtypeStruct((1,), jnp.float32),
        ),
        in_specs=[pl.BlockSpec(memory_space=pltpu.VMEM)] * 3 + [pl.BlockSpec(memory_space=pl.ANY)] * 3,
        out_specs=(pl.BlockSpec(memory_space=pltpu.VMEM), pl.BlockSpec(memory_space=pltpu.SMEM)),
        scratch_shapes=[
            pltpu.VMEM((n, 2, rows, width), jnp.bfloat16),
            pltpu.VMEM((n, 2, experts, rows), jnp.float32),
            pltpu.VMEM((local, width, units), jnp.bfloat16),
            pltpu.VMEM((local, width, units), jnp.bfloat16),
            pltpu.VMEM((local * units, width), jnp.bfloat16),
            pltpu.VMEM((2 * rows, local * units), jnp.bfloat16),
            pltpu.VMEM((n, chunks, 2, rows, span), jnp.bfloat16),
            block, block, block,
            pltpu.VMEM((rows, width), jnp.bfloat16),
            dma((3,)),
            dma((n, 2)), dma((n, 2)), dma((n, 2)), dma((n, 2)), dma((n,)), dma((n,)),
            dma((n, chunks)), dma((n, chunks)), dma((n, chunks)), dma((n, chunks)), dma, dma,
        ],
        compiler_params=pltpu.CompilerParams(
            collective_id=0, has_side_effects=True, vmem_limit_bytes=58 << 20
        ),
    )(tokens_in, ids.T, probs.T, gate_w, up_w, down_w.reshape(local * units, width))
    return handed, loss


def by_collectives(tokens_in, ids, probs, gate_w, up_w, down_w):
    axes = ("dp", "expert")
    local = gate_w.shape[0]
    groups = lax.axis_size("dp") * lax.axis_size("expert")
    rows, top = ids.shape
    experts = groups * local
    inputs = tokens_in.astype(jnp.float32)
    normed = (inputs * lax.rsqrt(jnp.mean(inputs * inputs, axis=-1, keepdims=True) + 1e-06)).astype(
        jnp.bfloat16
    )
    table = table_of(ids.T, probs.T, experts)
    tables = lax.all_gather(table, axes)
    gathered = lax.all_gather(normed, axes, tiled=True)
    first = lax.axis_index(axes) * local
    mine = lax.dynamic_slice_in_dim(tables, first, local, axis=1)

    def one_block(packed):
        tokens, weight = packed
        mixed = jnp.zeros(tokens.shape, jnp.float32)
        for e in range(local):
            gate = jnp.dot(tokens, gate_w[e], preferred_element_type=jnp.float32)
            lift = jnp.dot(tokens, up_w[e], preferred_element_type=jnp.float32)
            hidden = (jax.nn.silu(gate) * lift).astype(jnp.bfloat16)
            result = jnp.dot(hidden, down_w[e], preferred_element_type=jnp.float32)
            mixed = mixed + weight[e][:, None] * result
        return mixed.astype(jnp.bfloat16)

    partial = lax.map(one_block, (gathered.reshape(groups, rows, -1), mine))
    spread = lax.all_to_all(partial, axes, split_axis=0, concat_axis=0, tiled=True)
    mixture = jnp.sum(spread.astype(jnp.float32), axis=0)
    layer_out = (inputs + mixture).astype(jnp.bfloat16)
    counts = jnp.sum((tables > 0.0).astype(jnp.float32), axis=(0, 2))
    mass = jnp.sum(tables, axis=(0, 2))
    tokens_all = groups * rows
    loss = experts * jnp.sum(counts / (tokens_all * top) * (mass / tokens_all))
    sections = lax.axis_size("section")
    handed = lax.ppermute(layer_out, "section", [(s, (s + 1) % sections) for s in range(sections)])
    return handed, loss.reshape(1)


def per_device(stashed, expert_ids, route_probs, w_gate, w_up, w_down):
    n = lax.axis_size("expert")
    slots = 8 * n * stashed.shape[1] * stashed.shape[2] * stashed.dtype.itemsize
    weights = 3 * w_gate.size * w_gate.dtype.itemsize
    fits = slots + weights <= SLOTS_MAX_BYTES
    even = lax.axis_size("dp") == 2 and n % 2 == 0 and lax.axis_size("section") > 1
    layer = by_kernel if fits and even else by_collectives
    handed, loss = layer(stashed[0], expert_ids[0], route_probs[0], w_gate[0], w_up[0], w_down[0])
    return handed[None], loss


def solution(mesh):
    placed = P("section", ("dp", "expert"), None)
    weights = P("section", ("dp", "expert"), None, None)
    return jax.shard_map(
        per_device,
        mesh=mesh,
        in_specs=(placed, placed, placed, weights, weights, weights),
        out_specs=(placed, P("section")),
        check_vma=False,
    )
```

```python
import functools

import jax
import jax.numpy as jnp
from jax import lax
from jax.experimental import pallas as pl
from jax.experimental.pallas import tpu as pltpu
from jax.sharding import PartitionSpec as P

MESH = pl.DeviceIdType.MESH
SLOTS_MAX_BYTES = 48 << 20


def table_of(ids_t, probs_t, experts):
    weights = probs_t / jnp.sum(probs_t, axis=0, keepdims=True)
    labels = lax.broadcasted_iota(jnp.int32, (experts, ids_t.shape[1]), 0)
    table = jnp.zeros((experts, ids_t.shape[1]), jnp.float32)
    for k in range(ids_t.shape[0]):
        table = table + jnp.where(labels == ids_t[k : k + 1, :], weights[k : k + 1, :], 0.0)
    return table


def column_of(table, expert, rows):
    labels = lax.broadcasted_iota(jnp.int32, table.shape, 0)
    row = jnp.sum(jnp.where(labels == expert, table, 0.0), axis=0, keepdims=True)
    shape = (rows, table.shape[1])
    diagonal = lax.broadcasted_iota(jnp.int32, shape, 0) == lax.broadcasted_iota(jnp.int32, shape, 1)
    return jnp.sum(jnp.where(diagonal, row, 0.0), axis=1, keepdims=True)


def layer_kernel(
    n, sections, local, experts, tile,
    x_ref, ids_ref, probs_ref, wg_hbm, wu_hbm, wd_hbm,
    handed_ref, loss_ref,
    xg, cf, wg, wu, wd, hid, part, sib, red, got, xprev, total_out,
    w_sem, xs_sem, xr_sem, cs_sem, cr_sem, fs_sem, gs_sem,
    ps_sem, pr_sem, rs_sem, rr_sem, os_sem, or_sem,
):
    rows, width = x_ref.shape
    units = wg.shape[2]
    chunks, span = part.shape[1], part.shape[4]
    sec = lax.axis_index("section")
    c = lax.axis_index("dp")
    z = lax.axis_index("expert")
    other = 1 - c
    after = lax.rem(sec + 1, sections)
    before = lax.rem(sec + sections - 1, sections)
    me = c * n + z

    loads = []
    for number, (source, target) in enumerate(((wg_hbm, wg), (wu_hbm, wu), (wd_hbm, wd))):
        load = pltpu.make_async_copy(source, target, w_sem.at[number])
        load.start()
        loads.append(load)

    barrier = pltpu.get_barrier_semaphore()
    pl.semaphore_signal(barrier, inc=1, device_id=(sec, other, z), device_id_type=MESH)
    for b in range(n):
        pl.semaphore_signal(barrier, inc=1, device_id=(before, c, b), device_id_type=MESH)
    for step in range(1, n):
        pl.semaphore_signal(
            barrier, inc=1, device_id=(sec, c, lax.rem(z + step, n)), device_id_type=MESH
        )

    values = x_ref[...].astype(jnp.float32)
    scale = lax.rsqrt(jnp.mean(values * values, axis=-1, keepdims=True) + 1e-06)
    xg[z, c] = (values * scale).astype(jnp.bfloat16)
    cf[z, c] = table_of(ids_ref[...], probs_ref[...], experts)
    pl.semaphore_wait(barrier, 2 * n)

    def pair(b, target, x_send, c_send):
        slot = (b, c)
        return (
            pltpu.make_async_remote_copy(
                src_ref=xg.at[slot], dst_ref=xg.at[slot],
                send_sem=x_send, recv_sem=xr_sem.at[slot],
                device_id=target, device_id_type=MESH,
            ),
            pltpu.make_async_remote_copy(
                src_ref=cf.at[slot], dst_ref=cf.at[slot],
                send_sem=c_send, recv_sem=cr_sem.at[slot],
                device_id=target, device_id_type=MESH,
            ),
        )

    def up(b):
        return pair(b, (sec, c, z + 1), xs_sem.at[b, 0], cs_sem.at[b, 0])

    def down(b):
        return pair(b, (sec, c, z - 1), xs_sem.at[b, 1], cs_sem.at[b, 1])

    def across(b):
        return pair(b, (sec, other, z), fs_sem.at[b], gs_sem.at[b])

    def goes_up(b):
        return (b <= z) & (z < n - 1)

    def goes_down(b):
        return (b >= z) & (z > 0)

    def start_all(copies):
        for copy in copies:
            copy.start()

    def arrived(b, side):
        slot = (b, side)
        pltpu.make_async_remote_copy(
            src_ref=xg.at[slot], dst_ref=xg.at[slot], send_sem=fs_sem.at[0],
            recv_sem=xr_sem.at[slot], device_id=(sec, other, z), device_id_type=MESH,
        ).wait_recv()
        pltpu.make_async_remote_copy(
            src_ref=cf.at[slot], dst_ref=cf.at[slot], send_sem=gs_sem.at[0],
            recv_sem=cr_sem.at[slot], device_id=(sec, other, z), device_id_type=MESH,
        ).wait_recv()

    def forward(b):
        @pl.when(goes_up(b))
        def _():
            start_all(up(b))

        @pl.when(goes_down(b))
        def _():
            start_all(down(b))

        start_all(across(b))

    mirrored = z // (n // 2)
    near = z + mirrored * (n - 1 - 2 * z)

    def block_at(i):
        if i == 0:
            place = near
        else:
            step = (i + 1) // 2
            early = near - step if i % 2 else near + step
            inside = (i <= 2 * near).astype(jnp.int32)
            place = inside * early + (1 - inside) * i
        return place + mirrored * (n - 1 - 2 * place)

    def to_sibling(b, q):
        return pltpu.make_async_remote_copy(
            src_ref=part.at[b, q, other], dst_ref=sib.at[b, q],
            send_sem=ps_sem.at[b, q], recv_sem=pr_sem.at[b, q],
            device_id=(sec, other, z), device_id_type=MESH,
        )

    def onward(b, q):
        rise, fall = (b > z).astype(jnp.int32), (b < z).astype(jnp.int32)
        place = z + rise - fall
        last = (b == place).astype(jnp.int32)
        slot = last * ((1 - rise - fall) * z + rise * n + fall * (n + 1)) + (1 - last) * b
        return pltpu.make_async_remote_copy(
            src_ref=red.at[b, q], dst_ref=got.at[slot, q],
            send_sem=rs_sem.at[b, q], recv_sem=rr_sem.at[slot, q],
            device_id=(sec + last * (after - sec), c, place), device_id_type=MESH,
        )

    def received(slot, q):
        pltpu.make_async_remote_copy(
            src_ref=red.at[0, q], dst_ref=got.at[slot, q],
            send_sem=rs_sem.at[0, q], recv_sem=rr_sem.at[slot, q],
            device_id=(after, c, z), device_id_type=MESH,
        ).wait_recv()

    inner = (z > 0) & (z < n - 1)

    def finish(b, q, mine):
        to_sibling(b, q).wait_recv()
        red[b, q] = (part[b, q, c].astype(jnp.float32) + sib[b, q].astype(jnp.float32)).astype(
            jnp.bfloat16
        )
        if mine:
            onward(b, q).start()
        else:

            @pl.when((z == 0) | (z == n - 1))
            def _():
                onward(b, q).start()

    residual = pltpu.make_async_remote_copy(
        src_ref=x_ref, dst_ref=xprev, send_sem=os_sem, recv_sem=or_sem,
        device_id=(after, c, z), device_id_type=MESH,
    )
    pending = None
    forward(z)
    residual.start()
    for i in range(n):
        b = block_at(i)
        if i > 0:
            arrived(b, c)
            forward(b)
        arrived(b, other)
        if i == 0:
            loads[0].wait()
            loads[1].wait()
        tokens = xg[b].reshape(2 * rows, width)
        for e in range(local):
            expert = me * local + e
            weight = jnp.concatenate(
                [column_of(cf[b, side], expert, rows) for side in range(2)], axis=0
            )

            @pl.loop(0, units // tile)
            def _(j):
                columns = pl.ds(pl.multiple_of(j * tile, tile), tile)
                gate = jnp.dot(tokens, wg[e, :, columns], preferred_element_type=jnp.float32)
                lift = jnp.dot(tokens, wu[e, :, columns], preferred_element_type=jnp.float32)
                kept = pl.ds(pl.multiple_of(e * units + j * tile, tile), tile)
                hid[:, kept] = (jax.nn.silu(gate) * lift * weight).astype(jnp.bfloat16)

            if pending is not None:
                finish(*pending)
                pending = None

        if i == 0:
            loads[2].wait()
        hidden = hid[...]

        for q in range(chunks):

            @pl.loop(0, span // tile)
            def _(j):
                source = pl.ds(pl.multiple_of(q * span + j * tile, tile), tile)
                columns = pl.ds(pl.multiple_of(j * tile, tile), tile)
                result = jnp.dot(hidden, wd[:, source], preferred_element_type=jnp.float32)
                part[b, q, :, :, columns] = result.astype(jnp.bfloat16).reshape(2, rows, tile)

            to_sibling(b, q).start()
            if pending is not None:
                finish(*pending)
            pending = (b, q, i == 0)

    finish(*pending)

    @pl.when(inner)
    def _():
        turns = [(i, q) for i in range(n - 1) for q in range(chunks)]
        turns.sort(key=lambda t: t[0] * chunks + t[1] - (chunks - 1.5) * (t[0] == n - 2))
        for i, q in turns:
            ahead = (i < n - 1 - near).astype(jnp.int32)
            place = ahead * (near + 1 + i) + (1 - ahead) * (n - 2 - i)
            b = place + mirrored * (n - 1 - 2 * place)
            received(b, q)
            red[b, q] = (red[b, q].astype(jnp.float32) + got[b, q].astype(jnp.float32)).astype(
                jnp.bfloat16
            )
            onward(b, q).start()

    total = jnp.zeros((experts, cf.shape[3]), jnp.float32)
    chosen = jnp.zeros((experts, cf.shape[3]), jnp.float32)
    for b in range(n):
        for side in range(2):
            total = total + cf[b, side]
            chosen = chosen + (cf[b, side] > 0.0).astype(jnp.float32)
    count = jnp.sum(chosen, axis=1, keepdims=True)
    mass = jnp.sum(total, axis=1, keepdims=True)
    tokens_all = 2 * n * rows
    picks = tokens_all * ids_ref.shape[0]
    loss_ref[0] = experts * jnp.sum(count / picks * (mass / tokens_all))

    residual.wait_recv()
    for q in range(chunks):
        columns = pl.ds(q * span, span)
        received(z, q)
        total_out[...] = xprev[:, columns].astype(jnp.float32) + got[z, q].astype(jnp.float32)

        @pl.when(z > 0)
        def _():
            received(n, q)
            total_out[...] += got[n, q].astype(jnp.float32)

        @pl.when(z < n - 1)
        def _():
            received(n + 1, q)
            total_out[...] += got[n + 1, q].astype(jnp.float32)

        handed_ref[:, columns] = total_out[...].astype(jnp.bfloat16)

    residual.wait_send()
    for b in range(n):
        @pl.when(goes_up(b))
        def _():
            for copy in up(b):
                copy.wait_send()

        @pl.when(goes_down(b))
        def _():
            for copy in down(b):
                copy.wait_send()

        for copy in across(b):
            copy.wait_send()
        for q in range(chunks):
            to_sibling(b, q).wait_send()
            onward(b, q).wait_send()


def by_kernel(tokens_in, ids, probs, gate_w, up_w, down_w):
    n = lax.axis_size("expert")
    sections = lax.axis_size("section")
    local, width, units = gate_w.shape
    rows, top = ids.shape
    experts = 2 * n * local
    tile = 256 if units % 256 == 0 and width % 256 == 0 else 128
    chunks = 4 if width % (4 * tile) == 0 else 1
    span = width // chunks
    dma = pltpu.SemaphoreType.DMA
    block = pltpu.VMEM((n, chunks, rows, span), jnp.bfloat16)
    handed, loss = pl.pallas_call(
        functools.partial(layer_kernel, n, sections, local, experts, tile),
        out_shape=(
            jax.ShapeDtypeStruct((rows, width), jnp.bfloat16),
            jax.ShapeDtypeStruct((1,), jnp.float32),
        ),
        in_specs=[pl.BlockSpec(memory_space=pltpu.VMEM)] * 3 + [pl.BlockSpec(memory_space=pl.ANY)] * 3,
        out_specs=(pl.BlockSpec(memory_space=pltpu.VMEM), pl.BlockSpec(memory_space=pltpu.SMEM)),
        scratch_shapes=[
            pltpu.VMEM((n, 2, rows, width), jnp.bfloat16),
            pltpu.VMEM((n, 2, experts, rows), jnp.float32),
            pltpu.VMEM((local, width, units), jnp.bfloat16),
            pltpu.VMEM((local, width, units), jnp.bfloat16),
            pltpu.VMEM((local * units, width), jnp.bfloat16),
            pltpu.VMEM((2 * rows, local * units), jnp.bfloat16),
            pltpu.VMEM((n, chunks, 2, rows, span), jnp.bfloat16),
            block, block,
            pltpu.VMEM((n + 2, chunks, rows, span), jnp.bfloat16),
            pltpu.VMEM((rows, width), jnp.bfloat16),
            pltpu.VMEM((rows, span), jnp.float32),
            dma((3,)),
            dma((n, 2)), dma((n, 2)), dma((n, 2)), dma((n, 2)), dma((n,)), dma((n,)),
            dma((n, chunks)), dma((n, chunks)), dma((n, chunks)), dma((n + 2, chunks)), dma, dma,
        ],
        compiler_params=pltpu.CompilerParams(
            collective_id=0, has_side_effects=True, vmem_limit_bytes=58 << 20
        ),
    )(tokens_in, ids.T, probs.T, gate_w, up_w, down_w.reshape(local * units, width))
    return handed, loss


def by_collectives(tokens_in, ids, probs, gate_w, up_w, down_w):
    axes = ("dp", "expert")
    local = gate_w.shape[0]
    groups = lax.axis_size("dp") * lax.axis_size("expert")
    rows, top = ids.shape
    experts = groups * local
    inputs = tokens_in.astype(jnp.float32)
    normed = (inputs * lax.rsqrt(jnp.mean(inputs * inputs, axis=-1, keepdims=True) + 1e-06)).astype(
        jnp.bfloat16
    )
    table = table_of(ids.T, probs.T, experts)
    tables = lax.all_gather(table, axes)
    gathered = lax.all_gather(normed, axes, tiled=True)
    first = lax.axis_index(axes) * local
    mine = lax.dynamic_slice_in_dim(tables, first, local, axis=1)

    def one_block(packed):
        tokens, weight = packed
        mixed = jnp.zeros(tokens.shape, jnp.float32)
        for e in range(local):
            gate = jnp.dot(tokens, gate_w[e], preferred_element_type=jnp.float32)
            lift = jnp.dot(tokens, up_w[e], preferred_element_type=jnp.float32)
            hidden = (jax.nn.silu(gate) * lift).astype(jnp.bfloat16)
            result = jnp.dot(hidden, down_w[e], preferred_element_type=jnp.float32)
            mixed = mixed + weight[e][:, None] * result
        return mixed.astype(jnp.bfloat16)

    partial = lax.map(one_block, (gathered.reshape(groups, rows, -1), mine))
    spread = lax.all_to_all(partial, axes, split_axis=0, concat_axis=0, tiled=True)
    mixture = jnp.sum(spread.astype(jnp.float32), axis=0)
    layer_out = (inputs + mixture).astype(jnp.bfloat16)
    counts = jnp.sum((tables > 0.0).astype(jnp.float32), axis=(0, 2))
    mass = jnp.sum(tables, axis=(0, 2))
    tokens_all = groups * rows
    loss = experts * jnp.sum(counts / (tokens_all * top) * (mass / tokens_all))
    sections = lax.axis_size("section")
    handed = lax.ppermute(layer_out, "section", [(s, (s + 1) % sections) for s in range(sections)])
    return handed, loss.reshape(1)


def per_device(stashed, expert_ids, route_probs, w_gate, w_up, w_down):
    n = lax.axis_size("expert")
    slots = 8 * n * stashed.shape[1] * stashed.shape[2] * stashed.dtype.itemsize
    weights = 3 * w_gate.size * w_gate.dtype.itemsize
    fits = slots + weights <= SLOTS_MAX_BYTES
    even = lax.axis_size("dp") == 2 and n % 2 == 0 and lax.axis_size("section") > 1
    layer = by_kernel if fits and even else by_collectives
    handed, loss = layer(stashed[0], expert_ids[0], route_probs[0], w_gate[0], w_up[0], w_down[0])
    return handed[None], loss


def solution(mesh):
    placed = P("section", ("dp", "expert"), None)
    weights = P("section", ("dp", "expert"), None, None)
    return jax.shard_map(
        per_device,
        mesh=mesh,
        in_specs=(placed, placed, placed, weights, weights, weights),
        out_specs=(placed, P("section")),
        check_vma=False,
    )
```

```python
import functools

import jax
import jax.numpy as jnp
from jax import lax
from jax.experimental import pallas as pl
from jax.experimental.pallas import tpu as pltpu
from jax.sharding import PartitionSpec as P

MESH = pl.DeviceIdType.MESH
SLOTS_MAX_BYTES = 48 << 20
LAG = 2


def table_of(ids_t, probs_t, experts):
    weights = probs_t / jnp.sum(probs_t, axis=0, keepdims=True)
    labels = lax.broadcasted_iota(jnp.int32, (experts, ids_t.shape[1]), 0)
    table = jnp.zeros((experts, ids_t.shape[1]), jnp.float32)
    for k in range(ids_t.shape[0]):
        table = table + jnp.where(labels == ids_t[k : k + 1, :], weights[k : k + 1, :], 0.0)
    return table


def column_of(table, expert, rows):
    labels = lax.broadcasted_iota(jnp.int32, table.shape, 0)
    row = jnp.sum(jnp.where(labels == expert, table, 0.0), axis=0, keepdims=True)
    shape = (rows, table.shape[1])
    diagonal = lax.broadcasted_iota(jnp.int32, shape, 0) == lax.broadcasted_iota(jnp.int32, shape, 1)
    return jnp.sum(jnp.where(diagonal, row, 0.0), axis=1, keepdims=True)


def layer_kernel(
    n, sections, local, experts, tile,
    x_ref, ids_ref, probs_ref, wg_hbm, wu_hbm, wd_hbm,
    handed_ref, loss_ref,
    xg, cf, wg, wu, wd, hid, part, sib, red, got, xprev, total_out,
    w_sem, xs_sem, xr_sem, cs_sem, cr_sem, fs_sem, gs_sem,
    ps_sem, pr_sem, rs_sem, rr_sem, os_sem, or_sem,
):
    rows, width = x_ref.shape
    units = wg.shape[2]
    chunks, span = part.shape[1], part.shape[4]
    sec = lax.axis_index("section")
    c = lax.axis_index("dp")
    z = lax.axis_index("expert")
    other = 1 - c
    after = lax.rem(sec + 1, sections)
    before = lax.rem(sec + sections - 1, sections)
    me = c * n + z

    loads = []
    for number, (source, target) in enumerate(((wg_hbm, wg), (wu_hbm, wu), (wd_hbm, wd))):
        load = pltpu.make_async_copy(source, target, w_sem.at[number])
        load.start()
        loads.append(load)

    barrier = pltpu.get_barrier_semaphore()
    pl.semaphore_signal(barrier, inc=1, device_id=(sec, other, z), device_id_type=MESH)
    for b in range(n):
        pl.semaphore_signal(barrier, inc=1, device_id=(before, c, b), device_id_type=MESH)
    for step in range(1, n):
        pl.semaphore_signal(
            barrier, inc=1, device_id=(sec, c, lax.rem(z + step, n)), device_id_type=MESH
        )

    values = x_ref[...].astype(jnp.float32)
    scale = lax.rsqrt(jnp.mean(values * values, axis=-1, keepdims=True) + 1e-06)
    xg[z, c] = (values * scale).astype(jnp.bfloat16)
    cf[z, c] = table_of(ids_ref[...], probs_ref[...], experts)
    pl.semaphore_wait(barrier, 2 * n)

    def pair(b, target, x_send, c_send):
        slot = (b, c)
        return (
            pltpu.make_async_remote_copy(
                src_ref=xg.at[slot], dst_ref=xg.at[slot],
                send_sem=x_send, recv_sem=xr_sem.at[slot],
                device_id=target, device_id_type=MESH,
            ),
            pltpu.make_async_remote_copy(
                src_ref=cf.at[slot], dst_ref=cf.at[slot],
                send_sem=c_send, recv_sem=cr_sem.at[slot],
                device_id=target, device_id_type=MESH,
            ),
        )

    def up(b):
        return pair(b, (sec, c, z + 1), xs_sem.at[b, 0], cs_sem.at[b, 0])

    def down(b):
        return pair(b, (sec, c, z - 1), xs_sem.at[b, 1], cs_sem.at[b, 1])

    def across(b):
        return pair(b, (sec, other, z), fs_sem.at[b], gs_sem.at[b])

    def goes_up(b):
        return (b <= z) & (z < n - 1)

    def goes_down(b):
        return (b >= z) & (z > 0)

    def start_all(copies):
        for copy in copies:
            copy.start()

    def arrived(b, side):
        slot = (b, side)
        pltpu.make_async_remote_copy(
            src_ref=xg.at[slot], dst_ref=xg.at[slot], send_sem=fs_sem.at[0],
            recv_sem=xr_sem.at[slot], device_id=(sec, other, z), device_id_type=MESH,
        ).wait_recv()
        pltpu.make_async_remote_copy(
            src_ref=cf.at[slot], dst_ref=cf.at[slot], send_sem=gs_sem.at[0],
            recv_sem=cr_sem.at[slot], device_id=(sec, other, z), device_id_type=MESH,
        ).wait_recv()

    def forward(b):
        @pl.when(goes_up(b))
        def _():
            start_all(up(b))

        @pl.when(goes_down(b))
        def _():
            start_all(down(b))

        start_all(across(b))

    mirrored = z // (n // 2)
    near = z + mirrored * (n - 1 - 2 * z)

    def block_at(i):
        if i == 0:
            place = near
        else:
            step = (i + 1) // 2
            early = near - step if i % 2 else near + step
            inside = (i <= 2 * near).astype(jnp.int32)
            place = inside * early + (1 - inside) * i
        return place + mirrored * (n - 1 - 2 * place)

    def to_sibling(b, q):
        return pltpu.make_async_remote_copy(
            src_ref=part.at[b, q, other], dst_ref=sib.at[b, q],
            send_sem=ps_sem.at[b, q], recv_sem=pr_sem.at[b, q],
            device_id=(sec, other, z), device_id_type=MESH,
        )

    def onward(b, q):
        rise, fall = (b > z).astype(jnp.int32), (b < z).astype(jnp.int32)
        place = z + rise - fall
        last = (b == place).astype(jnp.int32)
        slot = last * ((1 - rise - fall) * z + rise * n + fall * (n + 1)) + (1 - last) * b
        return pltpu.make_async_remote_copy(
            src_ref=red.at[b, q], dst_ref=got.at[slot, q],
            send_sem=rs_sem.at[b, q], recv_sem=rr_sem.at[slot, q],
            device_id=(sec + last * (after - sec), c, place), device_id_type=MESH,
        )

    def received(slot, q):
        pltpu.make_async_remote_copy(
            src_ref=red.at[0, q], dst_ref=got.at[slot, q],
            send_sem=rs_sem.at[0, q], recv_sem=rr_sem.at[slot, q],
            device_id=(after, c, z), device_id_type=MESH,
        ).wait_recv()

    inner = (z > 0) & (z < n - 1)

    def finish(b, q, mine):
        to_sibling(b, q).wait_recv()
        red[b, q] = (part[b, q, c].astype(jnp.float32) + sib[b, q].astype(jnp.float32)).astype(
            jnp.bfloat16
        )
        if mine:
            onward(b, q).start()
        else:

            @pl.when((z == 0) | (z == n - 1))
            def _():
                onward(b, q).start()

    residual = pltpu.make_async_remote_copy(
        src_ref=x_ref, dst_ref=xprev, send_sem=os_sem, recv_sem=or_sem,
        device_id=(after, c, z), device_id_type=MESH,
    )
    pending = []
    forward(z)
    residual.start()
    for i in range(n):
        b = block_at(i)
        if i > 0:
            arrived(b, c)
            forward(b)
        arrived(b, other)
        if i == 0:
            loads[0].wait()
            loads[1].wait()
        tokens = xg[b].reshape(2 * rows, width)
        for e in range(local):
            expert = me * local + e
            weight = jnp.concatenate(
                [column_of(cf[b, side], expert, rows) for side in range(2)], axis=0
            )

            @pl.loop(0, units // tile)
            def _(j):
                columns = pl.ds(pl.multiple_of(j * tile, tile), tile)
                gate = jnp.dot(tokens, wg[e, :, columns], preferred_element_type=jnp.float32)
                lift = jnp.dot(tokens, wu[e, :, columns], preferred_element_type=jnp.float32)
                kept = pl.ds(pl.multiple_of(e * units + j * tile, tile), tile)
                hid[:, kept] = (jax.nn.silu(gate) * lift * weight).astype(jnp.bfloat16)

            while pending:
                finish(*pending.pop(0))

        if i == 0:
            loads[2].wait()
        hidden = hid[...]

        for q in range(chunks):

            @pl.loop(0, span // tile)
            def _(j):
                source = pl.ds(pl.multiple_of(q * span + j * tile, tile), tile)
                columns = pl.ds(pl.multiple_of(j * tile, tile), tile)
                result = jnp.dot(hidden, wd[:, source], preferred_element_type=jnp.float32)
                part[b, q, :, :, columns] = result.astype(jnp.bfloat16).reshape(2, rows, tile)

            to_sibling(b, q).start()
            pending.append((b, q, i == 0))
            if len(pending) > LAG:
                finish(*pending.pop(0))

    while pending:
        finish(*pending.pop(0))

    total = jnp.zeros((experts, cf.shape[3]), jnp.float32)
    chosen = jnp.zeros((experts, cf.shape[3]), jnp.float32)
    for b in range(n):
        for side in range(2):
            total = total + cf[b, side]
            chosen = chosen + (cf[b, side] > 0.0).astype(jnp.float32)
    count = jnp.sum(chosen, axis=1, keepdims=True)
    mass = jnp.sum(total, axis=1, keepdims=True)
    tokens_all = 2 * n * rows
    picks = tokens_all * ids_ref.shape[0]
    loss_ref[0] = experts * jnp.sum(count / picks * (mass / tokens_all))

    @pl.when(inner)
    def _():
        turns = [(i, q) for i in range(n - 1) for q in range(chunks)]
        turns.sort(key=lambda t: t[0] * chunks + t[1] - (chunks - 1.5) * (t[0] == n - 2))
        for i, q in turns:
            ahead = (i < n - 1 - near).astype(jnp.int32)
            place = ahead * (near + 1 + i) + (1 - ahead) * (n - 2 - i)
            b = place + mirrored * (n - 1 - 2 * place)
            received(b, q)
            red[b, q] = (red[b, q].astype(jnp.float32) + got[b, q].astype(jnp.float32)).astype(
                jnp.bfloat16
            )
            onward(b, q).start()

    residual.wait_recv()
    for q in range(chunks):
        columns = pl.ds(q * span, span)
        received(z, q)
        total_out[...] = xprev[:, columns].astype(jnp.float32) + got[z, q].astype(jnp.float32)

        @pl.when(z > 0)
        def _():
            received(n, q)
            total_out[...] += got[n, q].astype(jnp.float32)

        @pl.when(z < n - 1)
        def _():
            received(n + 1, q)
            total_out[...] += got[n + 1, q].astype(jnp.float32)

        handed_ref[:, columns] = total_out[...].astype(jnp.bfloat16)

    residual.wait_send()
    for b in range(n):
        @pl.when(goes_up(b))
        def _():
            for copy in up(b):
                copy.wait_send()

        @pl.when(goes_down(b))
        def _():
            for copy in down(b):
                copy.wait_send()

        for copy in across(b):
            copy.wait_send()
        for q in range(chunks):
            to_sibling(b, q).wait_send()
            onward(b, q).wait_send()


def by_kernel(tokens_in, ids, probs, gate_w, up_w, down_w):
    n = lax.axis_size("expert")
    sections = lax.axis_size("section")
    local, width, units = gate_w.shape
    rows, top = ids.shape
    experts = 2 * n * local
    tile = 256 if units % 256 == 0 and width % 256 == 0 else 128
    chunks = 8 if width % (8 * tile) == 0 else 1
    span = width // chunks
    dma = pltpu.SemaphoreType.DMA
    block = pltpu.VMEM((n, chunks, rows, span), jnp.bfloat16)
    handed, loss = pl.pallas_call(
        functools.partial(layer_kernel, n, sections, local, experts, tile),
        out_shape=(
            jax.ShapeDtypeStruct((rows, width), jnp.bfloat16),
            jax.ShapeDtypeStruct((1,), jnp.float32),
        ),
        in_specs=[pl.BlockSpec(memory_space=pltpu.VMEM)] * 3 + [pl.BlockSpec(memory_space=pl.ANY)] * 3,
        out_specs=(pl.BlockSpec(memory_space=pltpu.VMEM), pl.BlockSpec(memory_space=pltpu.SMEM)),
        scratch_shapes=[
            pltpu.VMEM((n, 2, rows, width), jnp.bfloat16),
            pltpu.VMEM((n, 2, experts, rows), jnp.float32),
            pltpu.VMEM((local, width, units), jnp.bfloat16),
            pltpu.VMEM((local, width, units), jnp.bfloat16),
            pltpu.VMEM((local * units, width), jnp.bfloat16),
            pltpu.VMEM((2 * rows, local * units), jnp.bfloat16),
            pltpu.VMEM((n, chunks, 2, rows, span), jnp.bfloat16),
            block, block,
            pltpu.VMEM((n + 2, chunks, rows, span), jnp.bfloat16),
            pltpu.VMEM((rows, width), jnp.bfloat16),
            pltpu.VMEM((rows, span), jnp.float32),
            dma((3,)),
            dma((n, 2)), dma((n, 2)), dma((n, 2)), dma((n, 2)), dma((n,)), dma((n,)),
            dma((n, chunks)), dma((n, chunks)), dma((n, chunks)), dma((n + 2, chunks)), dma, dma,
        ],
        compiler_params=pltpu.CompilerParams(
            collective_id=0, has_side_effects=True, vmem_limit_bytes=58 << 20
        ),
    )(tokens_in, ids.T, probs.T, gate_w, up_w, down_w.reshape(local * units, width))
    return handed, loss


def by_collectives(tokens_in, ids, probs, gate_w, up_w, down_w):
    axes = ("dp", "expert")
    local = gate_w.shape[0]
    groups = lax.axis_size("dp") * lax.axis_size("expert")
    rows, top = ids.shape
    experts = groups * local
    inputs = tokens_in.astype(jnp.float32)
    normed = (inputs * lax.rsqrt(jnp.mean(inputs * inputs, axis=-1, keepdims=True) + 1e-06)).astype(
        jnp.bfloat16
    )
    table = table_of(ids.T, probs.T, experts)
    tables = lax.all_gather(table, axes)
    gathered = lax.all_gather(normed, axes, tiled=True)
    first = lax.axis_index(axes) * local
    mine = lax.dynamic_slice_in_dim(tables, first, local, axis=1)

    def one_block(packed):
        tokens, weight = packed
        mixed = jnp.zeros(tokens.shape, jnp.float32)
        for e in range(local):
            gate = jnp.dot(tokens, gate_w[e], preferred_element_type=jnp.float32)
            lift = jnp.dot(tokens, up_w[e], preferred_element_type=jnp.float32)
            hidden = (jax.nn.silu(gate) * lift).astype(jnp.bfloat16)
            result = jnp.dot(hidden, down_w[e], preferred_element_type=jnp.float32)
            mixed = mixed + weight[e][:, None] * result
        return mixed.astype(jnp.bfloat16)

    partial = lax.map(one_block, (gathered.reshape(groups, rows, -1), mine))
    spread = lax.all_to_all(partial, axes, split_axis=0, concat_axis=0, tiled=True)
    mixture = jnp.sum(spread.astype(jnp.float32), axis=0)
    layer_out = (inputs + mixture).astype(jnp.bfloat16)
    counts = jnp.sum((tables > 0.0).astype(jnp.float32), axis=(0, 2))
    mass = jnp.sum(tables, axis=(0, 2))
    tokens_all = groups * rows
    loss = experts * jnp.sum(counts / (tokens_all * top) * (mass / tokens_all))
    sections = lax.axis_size("section")
    handed = lax.ppermute(layer_out, "section", [(s, (s + 1) % sections) for s in range(sections)])
    return handed, loss.reshape(1)


def per_device(stashed, expert_ids, route_probs, w_gate, w_up, w_down):
    n = lax.axis_size("expert")
    slots = 8 * n * stashed.shape[1] * stashed.shape[2] * stashed.dtype.itemsize
    weights = 3 * w_gate.size * w_gate.dtype.itemsize
    fits = slots + weights <= SLOTS_MAX_BYTES
    even = lax.axis_size("dp") == 2 and n % 2 == 0 and lax.axis_size("section") > 1
    layer = by_kernel if fits and even else by_collectives
    handed, loss = layer(stashed[0], expert_ids[0], route_probs[0], w_gate[0], w_up[0], w_down[0])
    return handed[None], loss


def solution(mesh):
    placed = P("section", ("dp", "expert"), None)
    weights = P("section", ("dp", "expert"), None, None)
    return jax.shard_map(
        per_device,
        mesh=mesh,
        in_specs=(placed, placed, placed, weights, weights, weights),
        out_specs=(placed, P("section")),
        check_vma=False,
    )
```
